32 devices in a mesh: section: 2 (over y), dp: 4 (over z), tensor: 4 (over x, core).
Axes of the slice: x: 2, y: 2, z: 4, core: 2. Of those that a mesh axis runs over, the one named last changes fastest.
Arguments:
- inputs: bfloat16 [2, 1536, 2048], P(None, ('dp', 'tensor')), may hold values from -6 to 6
- cotangent: bfloat16 [2, 1536, 2048], P(None, ('dp', 'tensor')), may hold values from -6 to 6
- attn_gain: bfloat16 [2, 2048], P('section', 'dp'), may hold values from 0.25 to 1.75
- mlp_gain: bfloat16 [2, 2048], P('section', 'dp'), may hold values from 0.25 to 1.75
- w_query: bfloat16 [2, 2048, 2048], P('section', 'dp', 'tensor'), may hold values from -0.125 to 0.125
- key_weight: bfloat16 [2, 2048, 512], P('section', 'dp', 'tensor'), may hold values from -0.125 to 0.125
- value_weight: bfloat16 [2, 2048, 512], P('section', 'dp', 'tensor'), may hold values from -0.125 to 0.125
- w_output: bfloat16 [2, 2048, 2048], P('section', 'dp', 'tensor'), may hold values from -2 to 2
- w_gate: bfloat16 [2, 2048, 8192], P('section', 'dp', 'tensor'), may hold values from -0.125 to 0.125
- w_up: bfloat16 [2, 2048, 8192], P('section', 'dp', 'tensor'), may hold values from -0.125 to 0.125
- w_down: bfloat16 [2, 2048, 8192], P('section', 'dp', 'tensor'), may hold values from -0.0625 to 0.0625
Outputs:
- section_out: bfloat16 [2, 2, 1536, 2048], P('section', None, ('dp', 'tensor'))
- section_in_grad: bfloat16 [2, 2, 1536, 2048], P('section', None, ('dp', 'tensor'))
- grad_attn_gain: float32 [2, 2048], P('section', 'dp')
- grad_mlp_gain: float32 [2, 2048], P('section', 'dp')
- grad_query: float32 [2, 2048, 2048], P('section', 'dp', 'tensor')
- grad_key: float32 [2, 2048, 512], P('section', 'dp', 'tensor')
- grad_value: float32 [2, 2048, 512], P('section', 'dp', 'tensor')
- grad_output: float32 [2, 2048, 2048], P('section', 'dp', 'tensor')
- grad_gate: float32 [2, 2048, 8192], P('section', 'dp', 'tensor')
- grad_up: float32 [2, 2048, 8192], P('section', 'dp', 'tensor')
- grad_down: float32 [2, 2048, 8192], P('section', 'dp', 'tensor')
The draws below stay inside these ranges and needn't reach their ends.
All inputs are finite; a program needn't handle non-finite values.
Results may differ from the reference program's by a relative error of at most 0.034.
Values may be sent and summed in bfloat16 or wider, within the bound.
No kernel may reach another device: no remote copies, remote signals or barrier semaphores. Data moves between devices by JAX's collectives and lax.ppermute only.
A program may use at most 256 MiB of HBM per device.

```python
import jax
import jax.numpy as jnp
from jax import lax

MODEL_WIDTH = 2048
FF = 8192
QUERY_HEADS = 32
KEY_VALUE_HEADS = 8
HEAD_WIDTH = 64
LEN = 384
MICRO = 2
TOKENS = 1536
N_DP = 4


def steps_of(own_key, dims, shards, low, largest):
    level, own = 1.0, jax.random.fold_in(own_key, 6)
    for axis_at, blocks in shards:
        steps = jnp.exp(jax.random.uniform(jax.random.fold_in(own, axis_at), (blocks,), jnp.float32, low / len(shards), largest / len(shards)))
        level = level * jnp.repeat(steps, dims[axis_at] // blocks).reshape([-1 if axis == axis_at else 1 for axis in range(len(dims))])
    return level


def bell_draw(own_key, shape, scale, limit, shards=(), kind=jnp.bfloat16):
    level = steps_of(own_key, shape, shards, -0.22, 0.18) if shards else 1.0
    result = jax.random.normal(own_key, shape, jnp.float32) * scale * level
    return jnp.minimum(jnp.maximum(result, -limit), limit).astype(kind)


def setup_inputs(seed: int = 0) -> dict:
    key_of = jax.random.split(jax.random.key(seed), 12)
    inputs = bell_draw(key_of[0], (MICRO, TOKENS, MODEL_WIDTH), 1.0, 6.0, ((1, 16),))
    cotangent = bell_draw(key_of[1], (MICRO, TOKENS, MODEL_WIDTH), 1.0, 6.0, ((1, 16),))
    attn_gain = jnp.clip(1.0 + 0.15 * jax.random.normal(key_of[2], (2, MODEL_WIDTH), jnp.float32), 0.25, 1.75).astype(jnp.bfloat16)
    mlp_gain = jnp.clip(1.0 + 0.15 * jax.random.normal(key_of[3], (2, MODEL_WIDTH), jnp.float32), 0.25, 1.75).astype(jnp.bfloat16)
    w_query = bell_draw(key_of[4], (2, MODEL_WIDTH, QUERY_HEADS * HEAD_WIDTH), MODEL_WIDTH ** -0.5, 0.125, ((0, 2), (1, 4), (2, 4)))
    key_weight = bell_draw(key_of[5], (2, MODEL_WIDTH, KEY_VALUE_HEADS * HEAD_WIDTH), MODEL_WIDTH ** -0.5, 0.125, ((0, 2), (1, 4), (2, 4)))
    value_weight = bell_draw(key_of[6], (2, MODEL_WIDTH, KEY_VALUE_HEADS * HEAD_WIDTH), MODEL_WIDTH ** -0.5, 0.125, ((0, 2), (1, 4), (2, 4)))
    w_output = bell_draw(key_of[7], (2, MODEL_WIDTH, QUERY_HEADS * HEAD_WIDTH), (2 * QUERY_HEADS * HEAD_WIDTH // LEN) ** -0.5, 2.0, ((0, 2), (1, 4), (2, 4)))
    w_gate = bell_draw(key_of[8], (2, MODEL_WIDTH, FF), MODEL_WIDTH ** -0.5, 0.125, ((0, 2), (1, 4), (2, 4)))
    w_up = bell_draw(key_of[9], (2, MODEL_WIDTH, FF), MODEL_WIDTH ** -0.5, 0.125, ((0, 2), (1, 4), (2, 4)))
    w_down = bell_draw(key_of[10], (2, MODEL_WIDTH, FF), FF ** -0.5, 0.0625, ((0, 2), (1, 4), (2, 4)))
    return {"inputs": inputs, "cotangent": cotangent, "attn_gain": attn_gain, "mlp_gain": mlp_gain, "w_query": w_query, "key_weight": key_weight, "value_weight": value_weight, "w_output": w_output, "w_gate": w_gate, "w_up": w_up, "w_down": w_down}


@jax.custom_vjp
def lower_section(v):
    return lax.optimization_barrier(v.astype(jnp.bfloat16)).astype(jnp.float32)

@jax.custom_vjp
def lower_section_backward(v):
    return v

def low_keep(v):
    return (lower_section(v), None)

def low_pass(kept, grad):
    return (grad,)

def back_keep(v):
    return (v, None)

def back_low(kept, grad):
    return (lower_section(grad),)
lower_section.defvjp(low_keep, low_pass)
lower_section_backward.defvjp(back_keep, back_low)
norm_eps = 1e-05
rope_base = 500000.0

def rope_tables(token_length, head_size):
    half = head_size // 2
    frequency = rope_base ** (-(jnp.arange(half, dtype=jnp.float32) * 2.0 / head_size))
    angles = jnp.arange(token_length, dtype=jnp.float32)[:, None] * frequency[None, :]
    return (jnp.cos(angles), jnp.sin(angles))

def rotate(values, cosine, sine):
    half = values.shape[-1] // 2
    cos_part = cosine[:, None, :]
    sin_part = sine[:, None, :]
    first = values[..., :half]
    second = values[..., half:]
    return jnp.concatenate([first * cos_part - second * sin_part, second * cos_part + first * sin_part], axis=-1)

def dense_matrix(left, right):
    return jnp.dot(left, right, precision=lax.Precision.HIGHEST)

def dense_last(left, right):
    return jnp.dot(left, right.T, precision=lax.Precision.HIGHEST)

def rms_scaled(rows, gain):
    return rows * lax.rsqrt(lax.optimization_barrier(jnp.mean(rows * rows, axis=-1, keepdims=True)) + norm_eps) * gain

def attend(triple):
    queries, key_rows, value_row_block = triple
    token_length = queries.shape[0]
    head_groups = QUERY_HEADS // KEY_VALUE_HEADS
    keys_all = jnp.repeat(key_rows, head_groups, axis=1)
    values_all = jnp.repeat(value_row_block, head_groups, axis=1)
    scores = lower_section_backward(jnp.einsum('qhd,khd->hqk', queries, keys_all, precision=lax.Precision.HIGHEST) * HEAD_WIDTH ** (-0.5))
    causal = jnp.arange(token_length)[:, None] >= jnp.arange(token_length)[None, :]
    scores = jnp.where(causal[None], scores, -1e+30)
    probs = lower_section(jax.nn.softmax(scores, axis=-1))
    mixed = jnp.einsum('hqk,khd->qhd', probs, values_all, precision=lax.Precision.HIGHEST)
    return lower_section_backward(lower_section(mixed))

def block(start, params):
    attn_gain, mlp_gain, w_query, key_weight, value_weight, w_output, w_gate, w_up, w_down = params
    tally_count, token_length, width = start.shape
    cosine, sine = rope_tables(token_length, HEAD_WIDTH)
    first_normalized = lower_section(rms_scaled(start, attn_gain)).reshape(tally_count * token_length, width)
    query_proj = lower_section_backward(dense_matrix(first_normalized, w_query)).reshape(tally_count, token_length, QUERY_HEADS, HEAD_WIDTH)
    key_projected = lower_section_backward(dense_matrix(first_normalized, key_weight)).reshape(tally_count, token_length, KEY_VALUE_HEADS, HEAD_WIDTH)
    queries = lower_section(rotate(query_proj, cosine, sine))
    key_rows = lower_section(rotate(key_projected, cosine, sine))
    value_row_block = lower_section(lower_section_backward(dense_matrix(first_normalized, value_weight))).reshape(tally_count, token_length, KEY_VALUE_HEADS, HEAD_WIDTH)
    mixed = lax.map(jax.checkpoint(attend), (queries, key_rows, value_row_block)).reshape(tally_count * token_length, QUERY_HEADS * HEAD_WIDTH)
    attn_branch = lower_section_backward(dense_last(mixed, w_output)).reshape(start.shape)
    middle = start + attn_branch
    normed_b = lower_section(rms_scaled(middle, mlp_gain)).reshape(tally_count * token_length, width)
    gate = lower_section_backward(dense_matrix(normed_b, w_gate))
    up_proj = lower_section_backward(dense_matrix(normed_b, w_up))
    hidden = lower_section(jax.nn.silu(gate) * up_proj)
    mlp_branch = lower_section_backward(dense_last(hidden, w_down)).reshape(start.shape)
    return lower_section_backward(lower_section(middle + mlp_branch))

def reference(inputs, cotangent, attn_gain, mlp_gain, w_query, key_weight, value_weight, w_output, w_gate, w_up, w_down):
    arrays = tuple((item.astype(jnp.float32) for item in (attn_gain, mlp_gain, w_query, key_weight, value_weight, w_output, w_gate, w_up, w_down)))
    first_params = tuple((item[0] for item in arrays))
    second_params = tuple((item[1] for item in arrays))
    shape = (MICRO * N_DP, LEN, MODEL_WIDTH)
    start = inputs.astype(jnp.float32).reshape(shape)
    middle, back_first = jax.vjp(block, start, first_params)
    final, back_second = jax.vjp(block, middle, second_params)
    grad_middle, grads_second = back_second(cotangent.astype(jnp.float32).reshape(shape))
    grad_start, grads_first = back_first(grad_middle)
    full = (2, MICRO, LEN * N_DP, MODEL_WIDTH)
    section_out = jnp.stack([middle, final]).reshape(full).astype(jnp.bfloat16)
    section_in_grad = jnp.stack([grad_start, grad_middle]).reshape(full).astype(jnp.bfloat16)
    grads = tuple((jnp.stack([one, two]) for one, two in zip(grads_first, grads_second)))
    return (section_out, section_in_grad, grads[0], grads[1], grads[2], grads[3], grads[4], grads[5], grads[6], grads[7], grads[8])
```

```python
import jax
import jax.numpy as jnp
from jax import lax
from jax.sharding import PartitionSpec as P

HEAD_WIDTH = 64
norm_eps = 1e-05
rope_base = 500000.0
GAIN_ROWS = 16
BF16 = jnp.bfloat16
F32 = jnp.float32


def swap(shard, axis, bit):
    length = lax.axis_size(axis)
    return lax.ppermute(shard, axis, [(i, i ^ bit) for i in range(length)])


def over_core(shard):
    return swap(shard, "tensor", 1)


def over_x(shard):
    return swap(shard, "tensor", 2)


def over_y(shard):
    return swap(shard, "section", 1)


def over_z(shard):
    return swap(shard, "dp", 1)


def rows_of(parts):
    return jnp.concatenate(parts, axis=0)


def product(left, right):
    return jnp.dot(left, right, preferred_element_type=F32)


def contract_last(left, right):
    return lax.dot_general(left, right, (((1,), (1,)), ((), ())), preferred_element_type=F32)


def contract_first(left, right):
    return lax.dot_general(left, right, (((0,), (0,)), ((), ())), preferred_element_type=F32)


def gather_eight(block):
    half = block.shape[0] // 2
    by_x = over_x(block)
    by_y = over_y(block)
    by_xy = rows_of([over_x(by_y[:half]), over_y(by_x[half:])])
    own = [block, by_x, by_y, by_xy]
    peer = [over_core(part) for part in own]
    return rows_of([own[0], peer[0], own[1], peer[1], own[2], peer[2], own[3], peer[3]])


def gather_eight_replicated(blocks):
    own = blocks.shape[0]
    wide = blocks.reshape(-1, blocks.shape[2])
    by_x = over_x(wide)
    peer = over_core(wide)
    peer_x = over_core(by_x)
    cut = blocks.shape[1]
    order = []
    for micro in range(own):
        piece = slice(micro * cut, (micro + 1) * cut)
        order += [wide[piece], peer[piece], by_x[piece], peer_x[piece]]
    return rows_of(order)


def scatter_eight(parts):
    size = parts.shape[0] // 8
    half = size // 2
    block = [parts[i * size : (i + 1) * size] for i in range(8)]
    kept = []
    for own, other in ((0, 1), (2, 3), (4, 5), (6, 7)):
        kept.append(block[own].astype(F32) + over_core(block[other]).astype(F32))
    mine, to_x, to_y, to_xy = kept
    to_xy = to_xy.astype(BF16)
    from_x = over_x(to_xy[:half]).astype(F32)
    from_y = over_y(to_xy[half:]).astype(F32)
    to_y = rows_of([to_y[:half] + from_x, to_y[half:]]).astype(BF16)
    to_x = rows_of([to_x[:half], to_x[half:] + from_y]).astype(BF16)
    return mine + over_x(to_x).astype(F32) + over_y(to_y).astype(F32)


def gather_sixteen(block, by_y=None):
    by_z = over_z(block)
    by_x = over_x(block)
    if by_y is None:
        by_y = over_y(block)
    by_zx = over_x(by_z)
    by_zy = over_y(by_z)
    by_xy = over_x(by_y)
    by_zxy = over_y(by_zx)
    own = [block, by_x, by_y, by_xy, by_z, by_zx, by_zy, by_zxy]
    peer = [over_core(part) for part in own]
    return rows_of(own + peer)


def scatter_sixteen(parts):
    size = parts.shape[0] // 16
    block = [parts[i * size : (i + 1) * size] for i in range(16)]
    kept = [
        block[i].astype(F32) + over_core(block[8 + i]).astype(F32) for i in range(8)
    ]
    mine, to_x, to_y, to_xy, to_z, to_zx, to_zy, to_zxy = kept
    to_y = to_y + over_x(to_xy.astype(BF16)).astype(F32)
    to_zx = to_zx + over_y(to_zxy.astype(BF16)).astype(F32)
    to_z = (
        to_z
        + over_x(to_zx.astype(BF16)).astype(F32)
        + over_y(to_zy.astype(BF16)).astype(F32)
    )
    return (
        mine
        + over_x(to_x.astype(BF16)).astype(F32)
        + over_y(to_y.astype(BF16)).astype(F32)
        + over_z(to_z.astype(BF16)).astype(F32)
    )


def pair_groups():
    length = lax.axis_size("dp")
    return [list(range(low, length, 2)) for low in range(2)]


def ordered(low, mine, other, axis):
    return jnp.where(
        low == 0,
        jnp.concatenate([mine, other], axis=axis),
        jnp.concatenate([other, mine], axis=axis),
    )


def gather_mlp(part):
    low = lax.axis_index("dp") & 1
    half = part.shape[1] // 2
    kept = lax.dynamic_slice_in_dim(part, low * half, half, 1)
    sent = lax.dynamic_slice_in_dim(part, (1 - low) * half, half, 1)
    part = ordered(low, kept, over_z(sent), 0)
    return lax.all_gather(part, "dp", axis=0, tiled=True, axis_index_groups=pair_groups())


def reduce_mlp(grad):
    low = lax.axis_index("dp") & 1
    part = lax.psum_scatter(
        grad, "dp", scatter_dimension=0, tiled=True, axis_index_groups=pair_groups()
    )
    half = part.shape[0] // 2
    kept = lax.dynamic_slice_in_dim(part, low * half, half, 0)
    sent = lax.dynamic_slice_in_dim(part, (1 - low) * half, half, 0)
    return ordered(low, kept, over_z(sent), 1)


def normalize(rows):
    inverse = lax.rsqrt(jnp.mean(rows * rows, axis=-1, keepdims=True) + norm_eps)
    return (rows * inverse, inverse)


def norm_back(grad_normed, unit, inverse, gain):
    scaled = grad_normed * gain
    return inverse * (scaled - unit * jnp.mean(scaled * unit, axis=-1, keepdims=True))


def rotate(values, cosine, sine, direction):
    half = values.shape[-1] // 2
    cos_part = cosine[:, None, :]
    sin_part = sine[:, None, :] * direction
    first = values[..., :half]
    second = values[..., half:]
    return jnp.concatenate(
        [first * cos_part - second * sin_part, second * cos_part + first * sin_part], axis=-1
    )


def attend_forward(qkv, tables):
    cosine, sine, mask, micro = tables
    rows = qkv.shape[0]
    token_length = rows // micro
    heads = (qkv.shape[1] - 2 * HEAD_WIDTH) // HEAD_WIDTH
    width = heads * HEAD_WIDTH
    q = qkv[:, :width].reshape(micro, token_length, heads, HEAD_WIDTH)
    k = qkv[:, width : width + HEAD_WIDTH].reshape(micro, token_length, 1, HEAD_WIDTH)
    values = qkv[:, width + HEAD_WIDTH :].astype(BF16).reshape(micro, token_length, HEAD_WIDTH)
    queries = rotate(q, cosine, sine, 1.0).astype(BF16)
    keys = rotate(k, cosine, sine, 1.0).astype(BF16)[:, :, 0]
    scores = (
        jnp.einsum("sqhd,skd->sqhk", queries, keys, preferred_element_type=F32)
        * HEAD_WIDTH ** (-0.5)
    )
    scores = jnp.where(mask[None, :, None, :], scores, -1e30)
    top = jnp.max(scores, axis=-1, keepdims=True)
    exped = jnp.exp(scores - top)
    probs = exped / jnp.sum(exped, axis=-1, keepdims=True)
    mixed = jnp.einsum("sqhk,skd->sqhd", probs.astype(BF16), values, preferred_element_type=F32)
    return mixed.astype(BF16).reshape(rows, width), (queries, keys, values, probs)


def attend_backward(kept, grad_mixed, tables):
    cosine, sine, mask, micro = tables
    queries, keys, values, probs = kept
    rows, width = grad_mixed.shape
    token_length = rows // micro
    scale = HEAD_WIDTH ** (-0.5)
    grad_mixed = grad_mixed.reshape(queries.shape)
    grad_probs = jnp.einsum("sqhd,skd->sqhk", grad_mixed, values, preferred_element_type=F32)
    delta = jnp.sum(grad_probs * probs, axis=-1, keepdims=True)
    grad_scores = (probs * (grad_probs - delta)).astype(BF16)
    grad_q = jnp.einsum("sqhk,skd->sqhd", grad_scores, keys, preferred_element_type=F32) * scale
    grad_k = jnp.einsum("sqhk,sqhd->skd", grad_scores, queries, preferred_element_type=F32) * scale
    grad_v = jnp.einsum(
        "sqhk,sqhd->skd", probs.astype(BF16), grad_mixed, preferred_element_type=F32
    )
    grad_q = rotate(grad_q, cosine, sine, -1.0).astype(BF16).reshape(rows, width)
    grad_k = rotate(grad_k[:, :, None], cosine, sine, -1.0).astype(BF16).reshape(rows, HEAD_WIDTH)
    grad_v = grad_v.astype(BF16).reshape(rows, HEAD_WIDTH)
    return jnp.concatenate([grad_q, grad_k, grad_v], axis=1)


def attention_half(start, rows_a, weights, tables):
    w_qkv, w_out = weights
    mixed, kept = attend_forward(product(rows_a, w_qkv), tables)
    branch = scatter_eight(contract_last(mixed, w_out).astype(BF16))
    return start + branch, (mixed, kept)


def per_device(
    inputs,
    cotangent,
    attn_gain,
    mlp_gain,
    w_query,
    key_weight,
    value_weight,
    w_output,
    w_gate,
    w_up,
    w_down,
):
    section = lax.axis_index("section")
    place = lax.axis_index("dp")
    first = section == 0
    micro, size, features = inputs.shape
    query_cols = w_query.shape[2] // 2
    key_cols = key_weight.shape[2] // 2

    query, key, value, output = w_query[0], key_weight[0], value_weight[0], w_output[0]
    gains = jnp.stack([attn_gain[0], mlp_gain[0]])
    cut = query_cols + 2 * key_cols
    width = cut + query_cols
    depth = query.shape[0]
    gains = jnp.pad(gains, ((0, GAIN_ROWS - 2), (0, width - depth)))

    def packed(columns, key_columns):
        parts = [query[:, columns], key[:, key_columns], value[:, key_columns], output[:, columns]]
        return rows_of([jnp.concatenate(parts, axis=1), gains])

    kept = packed(slice(0, query_cols), slice(0, key_cols))
    got = over_y(packed(slice(query_cols, None), slice(key_cols, None)))
    attention = [jnp.where(first, kept, got), jnp.where(first, got, kept)]
    mlp = [[], []]
    for weight in (w_gate[0], w_up[0], w_down[0]):
        half = weight.shape[1] // 2
        got = over_y(weight[:, half:])
        mlp[0].append(jnp.where(first, weight[:, :half], got))
        mlp[1].append(jnp.where(first, got, weight[:, :half]))
    full_attention = []
    full_mlp = []
    gains = []
    for index in range(2):
        whole = lax.all_gather(attention[index], "dp", axis=0, tiled=False)
        own = whole[:, :depth].reshape(features, width)
        full_attention.append((own[:, :cut], own[:, cut:]))
        gains.append(
            [whole[:, depth + row, :depth].reshape(features).astype(F32) for row in range(2)]
        )
        full_mlp.append([gather_mlp(part) for part in mlp[index]])

    quarter = lax.axis_index("tensor")
    positions = jnp.concatenate(
        [(quarter ^ other) * size + jnp.arange(size, dtype=jnp.int32) for other in range(4)]
    )
    head_half = HEAD_WIDTH // 2
    frequency = rope_base ** (-(jnp.arange(head_half, dtype=F32) * 2.0 / HEAD_WIDTH))
    angles = positions.astype(F32)[:, None] * frequency[None, :]
    mask = positions[:, None] >= positions[None, :]
    tables = (jnp.cos(angles), jnp.sin(angles), mask, micro)

    def own_first(pair):
        return jnp.where(first, pair, jnp.stack([pair[1], pair[0]]))

    both = own_first(inputs)
    both_out = own_first(cotangent)
    start = both[0].astype(F32)
    saved = []
    outputs = []
    for index in range(2):
        if index == 0:
            unit_a, inverse_a = normalize(start)
            unit_rows, _ = normalize(gather_eight_replicated(both).astype(F32))
            rows_a = (unit_rows * gains[0][0]).astype(BF16)
        else:
            unit_a, inverse_a = normalize(start)
            rows_a = gather_eight((unit_a * gains[index][0]).astype(BF16))
        middle, (mixed, attended) = attention_half(start, rows_a, full_attention[index], tables)
        unit_b, inverse_b = normalize(middle)
        rows_b = gather_sixteen((unit_b * gains[index][1]).astype(BF16))
        gate = product(rows_b, full_mlp[index][0])
        up = product(rows_b, full_mlp[index][1])
        hidden = (jax.nn.silu(gate) * up).astype(BF16)
        branch = scatter_sixteen(contract_last(hidden, full_mlp[index][2]).astype(BF16))
        result = (middle + branch).astype(BF16)
        outputs.append(result)
        start = result.astype(F32)
        saved.append(
            (unit_a, inverse_a, rows_a, mixed, attended, unit_b, inverse_b, rows_b, gate, up, hidden)
        )

    grad = both_out[0].astype(F32)
    out_rows = gather_sixteen(both_out[0], both_out[1])
    input_grads = [None, None]
    matrix = [None, None]
    gain_grads = [None, None]
    for index in (1, 0):
        unit_a, inverse_a, rows_a, mixed, attended, unit_b, inverse_b, rows_b, gate, up, hidden = (
            saved[index]
        )
        w_qkv, w_out = full_attention[index]
        weight_gate, weight_up, weight_down = full_mlp[index]
        if index == 0:
            out_rows = gather_sixteen(grad.astype(BF16))
        grad_down = reduce_mlp(contract_first(out_rows, hidden).astype(BF16))
        grad_hidden = product(out_rows, weight_down)
        sigmoid = jax.nn.sigmoid(gate)
        grad_gate = (grad_hidden * up * sigmoid * (1.0 + gate * (1.0 - sigmoid))).astype(BF16)
        grad_up = (grad_hidden * gate * sigmoid).astype(BF16)
        normed_part = contract_last(grad_gate, weight_gate) + contract_last(grad_up, weight_up)
        grad_wgate = reduce_mlp(contract_first(rows_b, grad_gate).astype(BF16))
        grad_wup = reduce_mlp(contract_first(rows_b, grad_up).astype(BF16))
        grad_normed_b = scatter_sixteen(normed_part.astype(BF16))
        gain_b = jnp.sum(grad_normed_b * unit_b, axis=0)
        grad_middle = grad + norm_back(grad_normed_b, unit_b, inverse_b, gains[index][1])
        branch_rows = gather_eight(grad_middle.astype(BF16))
        grad_woutput = contract_first(branch_rows, mixed).astype(BF16)
        grad_mixed = product(branch_rows, w_out).astype(BF16)
        grad_qkv = attend_backward(attended, grad_mixed, tables)
        grad_wqkv = contract_first(rows_a, grad_qkv).astype(BF16)
        grad_attention = lax.psum_scatter(
            jnp.concatenate([grad_wqkv, grad_woutput], axis=1),
            "dp",
            scatter_dimension=0,
            tiled=True,
        )
        grad_normed_a = scatter_eight(contract_last(grad_qkv, w_qkv).astype(BF16))
        gain_a = jnp.sum(grad_normed_a * unit_a, axis=0)
        grad_start = grad_middle + norm_back(grad_normed_a, unit_a, inverse_a, gains[index][0])
        sent = grad_start.astype(BF16)
        input_grads[index] = sent
        grad = sent.astype(F32)
        matrix[index] = [grad_attention, grad_wgate, grad_wup, grad_down]
        gain_grads[index] = jnp.stack([gain_a, gain_b])

    whole = []
    for one, two in zip(matrix[0], matrix[1]):
        got_one = lax.ppermute(one, "section", [(1, 0)])
        got_two = lax.ppermute(two, "section", [(0, 1)])
        whole.append((jnp.where(first, one, two), jnp.where(first, got_one, got_two)))
    sizes = (query_cols, key_cols, key_cols, query_cols)
    grads = []
    offset = 0
    for width in sizes:
        grads.append(
            jnp.concatenate(
                [part[:, offset : offset + width].astype(F32) for part in whole[0]], axis=1
            )
        )
        offset += width
    for pair in whole[1:]:
        grads.append(jnp.concatenate([part.astype(F32) for part in pair], axis=1))

    gain_sum = jnp.stack(gain_grads)
    gain_sum = jnp.where(first, gain_sum[0], gain_sum[1]) + over_y(
        jnp.where(first, gain_sum[1], gain_sum[0])
    )
    bit = lax.axis_size("dp") // 2
    while bit:
        half = gain_sum.shape[1] // 2
        high = (place & bit) > 0
        low_part, high_part = gain_sum[:, :half], gain_sum[:, half:]
        gain_sum = jnp.where(high, high_part, low_part) + swap(
            jnp.where(high, low_part, high_part), "dp", bit
        )
        bit //= 2
    gain_sum = gain_sum + over_x(gain_sum)
    gain_sum = gain_sum + over_core(gain_sum)

    def by_section(one, two):
        own = jnp.where(first, one, two)
        other = over_y(jnp.where(first, two, one))
        return jnp.where(first, jnp.stack([own, other]), jnp.stack([other, own]))[None]

    return (
        by_section(outputs[0], outputs[1]),
        by_section(input_grads[0], input_grads[1]),
        gain_sum[0][None],
        gain_sum[1][None],
    ) + tuple(grad[None] for grad in grads)


def solution(mesh):
    matrix = P("section", "dp", "tensor")
    tokens = P(None, ("dp", "tensor"), None)
    gain = P("section", "dp")
    result = P("section", None, ("dp", "tensor"), None)
    return jax.shard_map(
        per_device,
        mesh=mesh,
        in_specs=(tokens, tokens, gain, gain) + (matrix,) * 7,
        out_specs=(result, result, gain, gain) + (matrix,) * 7,
        check_vma=False,
    )
```

```python
import jax
import jax.numpy as jnp
from jax import lax
from jax.sharding import PartitionSpec as P

HEAD_WIDTH = 64
norm_eps = 1e-05
rope_base = 500000.0
GAIN_ROWS = 16
BF16 = jnp.bfloat16
F32 = jnp.float32


def swap(shard, axis, bit):
    length = lax.axis_size(axis)
    return lax.ppermute(shard, axis, [(i, i ^ bit) for i in range(length)])


def over_core(shard):
    return swap(shard, "tensor", 1)


def over_x(shard):
    return swap(shard, "tensor", 2)


def over_y(shard):
    return swap(shard, "section", 1)


def over_z(shard):
    return swap(shard, "dp", 1)


def after(value, *earlier):
    return lax.optimization_barrier((value, earlier))[0]


def rows_of(parts):
    return jnp.concatenate(parts, axis=0)


def product(left, right):
    return jnp.dot(left, right, preferred_element_type=F32)


def contract_last(left, right):
    return lax.dot_general(left, right, (((1,), (1,)), ((), ())), preferred_element_type=F32)


def contract_first(left, right):
    return lax.dot_general(left, right, (((0,), (0,)), ((), ())), preferred_element_type=F32)


def gather_eight(block):
    half = block.shape[0] // 2
    by_x = over_x(block)
    by_y = over_y(block)
    by_xy = rows_of([over_x(by_y[:half]), over_y(by_x[half:])])
    own = [block, by_x, by_y, by_xy]
    peer = [over_core(part) for part in own]
    return rows_of([own[0], peer[0], own[1], peer[1], own[2], peer[2], own[3], peer[3]])


def gather_eight_replicated(blocks):
    own = blocks.shape[0]
    wide = blocks.reshape(-1, blocks.shape[2])
    by_x = over_x(wide)
    peer = over_core(wide)
    peer_x = over_core(by_x)
    cut = blocks.shape[1]
    order = []
    for micro in range(own):
        piece = slice(micro * cut, (micro + 1) * cut)
        order += [wide[piece], peer[piece], by_x[piece], peer_x[piece]]
    return rows_of(order)


def scatter_eight(parts):
    size = parts.shape[0] // 8
    half = size // 2
    block = [parts[i * size : (i + 1) * size] for i in range(8)]
    kept = []
    for own, other in ((0, 1), (2, 3), (4, 5), (6, 7)):
        kept.append(block[own].astype(F32) + over_core(block[other]).astype(F32))
    mine, to_x, to_y, to_xy = kept
    to_xy = to_xy.astype(BF16)
    from_x = over_x(to_xy[:half]).astype(F32)
    from_y = over_y(to_xy[half:]).astype(F32)
    to_y = rows_of([to_y[:half] + from_x, to_y[half:]]).astype(BF16)
    to_x = rows_of([to_x[:half], to_x[half:] + from_y]).astype(BF16)
    return mine + over_x(to_x).astype(F32) + over_y(to_y).astype(F32)


def gather_sixteen(block, by_y=None):
    by_z = over_z(block)
    by_x = over_x(block)
    if by_y is None:
        by_y = over_y(block)
    by_zx = over_x(by_z)
    by_zy = over_y(by_z)
    by_xy = over_x(by_y)
    by_zxy = over_y(by_zx)
    own = [block, by_x, by_y, by_xy, by_z, by_zx, by_zy, by_zxy]
    peer = [over_core(part) for part in own]
    return rows_of(own + peer)


def scatter_sixteen(parts):
    size = parts.shape[0] // 16
    block = [parts[i * size : (i + 1) * size] for i in range(16)]
    kept = [
        block[i].astype(F32) + over_core(block[8 + i]).astype(F32) for i in range(8)
    ]
    mine, to_x, to_y, to_xy, to_z, to_zx, to_zy, to_zxy = kept
    to_y = to_y + over_x(to_xy.astype(BF16)).astype(F32)
    to_zx = to_zx + over_y(to_zxy.astype(BF16)).astype(F32)
    to_z = (
        to_z
        + over_x(to_zx.astype(BF16)).astype(F32)
        + over_y(to_zy.astype(BF16)).astype(F32)
    )
    return (
        mine
        + over_x(to_x.astype(BF16)).astype(F32)
        + over_y(to_y.astype(BF16)).astype(F32)
        + over_z(to_z.astype(BF16)).astype(F32)
    )


def pair_groups():
    length = lax.axis_size("dp")
    return [list(range(low, length, 2)) for low in range(2)]


def ordered(low, mine, other, axis):
    return jnp.where(
        low == 0,
        jnp.concatenate([mine, other], axis=axis),
        jnp.concatenate([other, mine], axis=axis),
    )


def exchange_mlp(part):
    low = lax.axis_index("dp") & 1
    half = part.shape[1] // 2
    kept = lax.dynamic_slice_in_dim(part, low * half, half, 1)
    sent = lax.dynamic_slice_in_dim(part, (1 - low) * half, half, 1)
    return ordered(low, kept, over_z(sent), 0)


def gather_mlp(part):
    return lax.all_gather(part, "dp", axis=0, tiled=True, axis_index_groups=pair_groups())


def reduce_mlp(grad):
    low = lax.axis_index("dp") & 1
    part = lax.psum_scatter(
        grad, "dp", scatter_dimension=0, tiled=True, axis_index_groups=pair_groups()
    )
    half = part.shape[0] // 2
    kept = lax.dynamic_slice_in_dim(part, low * half, half, 0)
    sent = lax.dynamic_slice_in_dim(part, (1 - low) * half, half, 0)
    return ordered(low, kept, over_z(sent), 1)


def normalize(rows):
    inverse = lax.rsqrt(jnp.mean(rows * rows, axis=-1, keepdims=True) + norm_eps)
    return (rows * inverse, inverse)


def norm_back(grad_normed, unit, inverse, gain):
    scaled = grad_normed * gain
    return inverse * (scaled - unit * jnp.mean(scaled * unit, axis=-1, keepdims=True))


def rotate(values, cosine, sine, direction):
    half = values.shape[-1] // 2
    cos_part = cosine[:, None, :]
    sin_part = sine[:, None, :] * direction
    first = values[..., :half]
    second = values[..., half:]
    return jnp.concatenate(
        [first * cos_part - second * sin_part, second * cos_part + first * sin_part], axis=-1
    )


def attend_forward(qkv, tables):
    cosine, sine, mask, micro = tables
    rows = qkv.shape[0]
    token_length = rows // micro
    heads = (qkv.shape[1] - 2 * HEAD_WIDTH) // HEAD_WIDTH
    width = heads * HEAD_WIDTH
    q = qkv[:, :width].reshape(micro, token_length, heads, HEAD_WIDTH)
    k = qkv[:, width : width + HEAD_WIDTH].reshape(micro, token_length, 1, HEAD_WIDTH)
    values = qkv[:, width + HEAD_WIDTH :].astype(BF16).reshape(micro, token_length, HEAD_WIDTH)
    queries = rotate(q, cosine, sine, 1.0).astype(BF16)
    keys = rotate(k, cosine, sine, 1.0).astype(BF16)[:, :, 0]
    scores = (
        jnp.einsum("sqhd,skd->sqhk", queries, keys, preferred_element_type=F32)
        * HEAD_WIDTH ** (-0.5)
    )
    scores = jnp.where(mask[None, :, None, :], scores, -1e30)
    top = jnp.max(scores, axis=-1, keepdims=True)
    exped = jnp.exp(scores - top)
    probs = exped / jnp.sum(exped, axis=-1, keepdims=True)
    mixed = jnp.einsum("sqhk,skd->sqhd", probs.astype(BF16), values, preferred_element_type=F32)
    return mixed.astype(BF16).reshape(rows, width), (queries, keys, values, probs)


def attend_backward(kept, grad_mixed, tables):
    cosine, sine, mask, micro = tables
    queries, keys, values, probs = kept
    rows, width = grad_mixed.shape
    token_length = rows // micro
    scale = HEAD_WIDTH ** (-0.5)
    grad_mixed = grad_mixed.reshape(queries.shape)
    grad_probs = jnp.einsum("sqhd,skd->sqhk", grad_mixed, values, preferred_element_type=F32)
    delta = jnp.sum(grad_probs * probs, axis=-1, keepdims=True)
    grad_scores = (probs * (grad_probs - delta)).astype(BF16)
    grad_q = jnp.einsum("sqhk,skd->sqhd", grad_scores, keys, preferred_element_type=F32) * scale
    grad_k = jnp.einsum("sqhk,sqhd->skd", grad_scores, queries, preferred_element_type=F32) * scale
    grad_v = jnp.einsum(
        "sqhk,sqhd->skd", probs.astype(BF16), grad_mixed, preferred_element_type=F32
    )
    grad_q = rotate(grad_q, cosine, sine, -1.0).astype(BF16).reshape(rows, width)
    grad_k = rotate(grad_k[:, :, None], cosine, sine, -1.0).astype(BF16).reshape(rows, HEAD_WIDTH)
    grad_v = grad_v.astype(BF16).reshape(rows, HEAD_WIDTH)
    return jnp.concatenate([grad_q, grad_k, grad_v], axis=1)


def attention_half(start, rows_a, weights, tables):
    w_qkv, w_out = weights
    mixed, kept = attend_forward(product(rows_a, w_qkv), tables)
    branch = scatter_eight(contract_last(mixed, w_out).astype(BF16))
    return start + branch, (mixed, kept)


def per_device(
    inputs,
    cotangent,
    attn_gain,
    mlp_gain,
    w_query,
    key_weight,
    value_weight,
    w_output,
    w_gate,
    w_up,
    w_down,
):
    section = lax.axis_index("section")
    place = lax.axis_index("dp")
    first = section == 0
    micro, size, features = inputs.shape
    query_cols = w_query.shape[2] // 2
    key_cols = key_weight.shape[2] // 2

    query, key, value, output = w_query[0], key_weight[0], value_weight[0], w_output[0]
    gains = jnp.stack([attn_gain[0], mlp_gain[0]])
    cut = query_cols + 2 * key_cols
    width = cut + query_cols
    depth = query.shape[0]
    gains = jnp.pad(gains, ((0, GAIN_ROWS - 2), (0, width - depth)))

    def packed(columns, key_columns):
        parts = [query[:, columns], key[:, key_columns], value[:, key_columns], output[:, columns]]
        return rows_of([jnp.concatenate(parts, axis=1), gains])

    kept = packed(slice(0, query_cols), slice(0, key_cols))
    got = over_y(packed(slice(query_cols, None), slice(key_cols, None)))
    attention = [jnp.where(first, kept, got), jnp.where(first, got, kept)]
    mlp = [[], []]
    for weight in (w_gate[0], w_up[0], w_down[0]):
        half = weight.shape[1] // 2
        got = over_y(weight[:, half:])
        mlp[0].append(jnp.where(first, weight[:, :half], got))
        mlp[1].append(jnp.where(first, got, weight[:, :half]))
    parts = [[exchange_mlp(part) for part in section_parts] for section_parts in mlp]
    full_attention = []
    full_mlp = []
    gains = []
    for index in range(2):
        whole = lax.all_gather(attention[index], "dp", axis=0, tiled=False)
        own = whole[:, :depth].reshape(features, width)
        full_attention.append((own[:, :cut], own[:, cut:]))
        gains.append(
            [whole[:, depth + row, :depth].reshape(features).astype(F32) for row in range(2)]
        )
        full_mlp.append([gather_mlp(part) for part in parts[index]])

    quarter = lax.axis_index("tensor")
    positions = jnp.concatenate(
        [(quarter ^ other) * size + jnp.arange(size, dtype=jnp.int32) for other in range(4)]
    )
    head_half = HEAD_WIDTH // 2
    frequency = rope_base ** (-(jnp.arange(head_half, dtype=F32) * 2.0 / HEAD_WIDTH))
    angles = positions.astype(F32)[:, None] * frequency[None, :]
    mask = positions[:, None] >= positions[None, :]
    tables = (jnp.cos(angles), jnp.sin(angles), mask, micro)

    def own_first(pair):
        return jnp.where(first, pair, jnp.stack([pair[1], pair[0]]))

    both = own_first(inputs)
    both_out = own_first(cotangent)
    start = both[0].astype(F32)
    saved = []
    outputs = []
    for index in range(2):
        if index == 0:
            unit_a, inverse_a = normalize(start)
            unit_rows, _ = normalize(gather_eight_replicated(both).astype(F32))
            rows_a = (unit_rows * gains[0][0]).astype(BF16)
        else:
            unit_a, inverse_a = normalize(start)
            rows_a = gather_eight((unit_a * gains[index][0]).astype(BF16))
        middle, (mixed, attended) = attention_half(start, rows_a, full_attention[index], tables)
        if index == 0:
            out_rows = gather_sixteen(both_out[0], both_out[1])
        else:
            middle = after(middle, out_rows)
        unit_b, inverse_b = normalize(middle)
        rows_b = gather_sixteen((unit_b * gains[index][1]).astype(BF16))
        gate = product(rows_b, full_mlp[index][0])
        up = product(rows_b, full_mlp[index][1])
        hidden = (jax.nn.silu(gate) * up).astype(BF16)
        part = contract_last(hidden, full_mlp[index][2]).astype(BF16)
        if index == 0:
            part = after(part, *parts[1])
        result = (middle + scatter_sixteen(part)).astype(BF16)
        outputs.append(result)
        start = result.astype(F32)
        saved.append(
            (unit_a, inverse_a, rows_a, mixed, attended, unit_b, inverse_b, rows_b, gate, up, hidden)
        )

    grad = both_out[0].astype(F32)
    input_grads = [None, None]
    matrix = [None, None]
    gain_grads = [None, None]
    for index in (1, 0):
        unit_a, inverse_a, rows_a, mixed, attended, unit_b, inverse_b, rows_b, gate, up, hidden = (
            saved[index]
        )
        w_qkv, w_out = full_attention[index]
        weight_gate, weight_up, weight_down = full_mlp[index]
        if index == 0:
            out_rows = gather_sixteen(grad.astype(BF16))
        grad_down = reduce_mlp(contract_first(out_rows, hidden).astype(BF16))
        grad_hidden = product(out_rows, weight_down)
        sigmoid = jax.nn.sigmoid(gate)
        grad_gate = (grad_hidden * up * sigmoid * (1.0 + gate * (1.0 - sigmoid))).astype(BF16)
        grad_up = (grad_hidden * gate * sigmoid).astype(BF16)
        normed_part = contract_last(grad_gate, weight_gate) + contract_last(grad_up, weight_up)
        grad_wgate = reduce_mlp(contract_first(rows_b, grad_gate).astype(BF16))
        grad_wup = reduce_mlp(contract_first(rows_b, grad_up).astype(BF16))
        grad_normed_b = scatter_sixteen(normed_part.astype(BF16))
        gain_b = jnp.sum(grad_normed_b * unit_b, axis=0)
        grad_middle = grad + norm_back(grad_normed_b, unit_b, inverse_b, gains[index][1])
        branch_rows = gather_eight(grad_middle.astype(BF16))
        grad_woutput = contract_first(branch_rows, mixed).astype(BF16)
        grad_mixed = product(branch_rows, w_out).astype(BF16)
        grad_qkv = attend_backward(attended, grad_mixed, tables)
        grad_wqkv = contract_first(rows_a, grad_qkv).astype(BF16)
        grad_attention = lax.psum_scatter(
            jnp.concatenate([grad_wqkv, grad_woutput], axis=1),
            "dp",
            scatter_dimension=0,
            tiled=True,
        )
        grad_normed_a = scatter_eight(contract_last(grad_qkv, w_qkv).astype(BF16))
        gain_a = jnp.sum(grad_normed_a * unit_a, axis=0)
        grad_start = grad_middle + norm_back(grad_normed_a, unit_a, inverse_a, gains[index][0])
        sent = grad_start.astype(BF16)
        input_grads[index] = sent
        grad = sent.astype(F32)
        matrix[index] = [grad_attention, grad_wgate, grad_wup, grad_down]
        gain_grads[index] = jnp.stack([gain_a, gain_b])

    whole = []
    for one, two in zip(matrix[0], matrix[1]):
        got_one = lax.ppermute(one, "section", [(1, 0)])
        got_two = lax.ppermute(two, "section", [(0, 1)])
        whole.append((jnp.where(first, one, two), jnp.where(first, got_one, got_two)))
    sizes = (query_cols, key_cols, key_cols, query_cols)
    grads = []
    offset = 0
    for width in sizes:
        grads.append(
            jnp.concatenate(
                [part[:, offset : offset + width].astype(F32) for part in whole[0]], axis=1
            )
        )
        offset += width
    for pair in whole[1:]:
        grads.append(jnp.concatenate([part.astype(F32) for part in pair], axis=1))

    gain_sum = jnp.stack(gain_grads)
    gain_sum = jnp.where(first, gain_sum[0], gain_sum[1]) + over_y(
        jnp.where(first, gain_sum[1], gain_sum[0])
    )
    bit = lax.axis_size("dp") // 2
    while bit:
        half = gain_sum.shape[1] // 2
        high = (place & bit) > 0
        low_part, high_part = gain_sum[:, :half], gain_sum[:, half:]
        gain_sum = jnp.where(high, high_part, low_part) + swap(
            jnp.where(high, low_part, high_part), "dp", bit
        )
        bit //= 2
    gain_sum = gain_sum + over_x(gain_sum)
    gain_sum = gain_sum + over_core(gain_sum)

    def by_section(one, two):
        own = jnp.where(first, one, two)
        other = over_y(jnp.where(first, two, one))
        return jnp.where(first, jnp.stack([own, other]), jnp.stack([other, own]))[None]

    return (
        by_section(outputs[0], outputs[1]),
        by_section(input_grads[0], input_grads[1]),
        gain_sum[0][None],
        gain_sum[1][None],
    ) + tuple(grad[None] for grad in grads)


def solution(mesh):
    matrix = P("section", "dp", "tensor")
    tokens = P(None, ("dp", "tensor"), None)
    gain = P("section", "dp")
    result = P("section", None, ("dp", "tensor"), None)
    return jax.shard_map(
        per_device,
        mesh=mesh,
        in_specs=(tokens, tokens, gain, gain) + (matrix,) * 7,
        out_specs=(result, result, gain, gain) + (matrix,) * 7,
        check_vma=False,
    )
```
